32 devices in a mesh: az: 8 (over z, y), rad: 4 (over x, core).
Axes of the slice: x: 2, y: 2, z: 4, core: 2. Of those that a mesh axis runs over, the one named last changes fastest.
Arguments:
- combustor_state: float32 [9, 16, 32, 1024], P(None, None, 'rad', 'az'), may hold values from -6 to 6
- swirl_speed: float32 [16, 32, 1024], P(None, 'rad', 'az'), may hold values from -0.6 to 1
- reaction_rate: float32 [16, 32, 1024], P(None, 'rad', 'az'), may hold values from 0.1 to 1
- kinetics: float32 [9, 9], replicated, may hold values from -2 to 2
- stator_state: float32 [9, 16, 32, 2048], P(None, None, 'rad', 'az'), may hold values from -6 to 6
- inlet_index: int32 [8, 256], P('az'), may hold values from 0 to 254, as said below
- inlet_weight: float32 [8, 256], P('az'), may hold values from 0 to 1
Outputs:
- combustor_next: float32 [9, 16, 32, 1024], P(None, None, 'rad', 'az')
- stator_next: float32 [9, 16, 32, 2048], P(None, None, 'rad', 'az')
The draws below stay inside these ranges and needn't reach their ends.
Inputs may be any that keep to these rules, and one draw needn't show every extreme that they name: Along j, inlet_index[p, j] never falls and rises by at most one from one pitch cell to the next.
All inputs are finite; a program needn't handle non-finite values.
Results may differ from the reference program's by a relative error of at most 0.0003.
Values sent between devices are 32-bit elements; how exact they have to be, the bound alone decides.
A program may use at most 64 MiB of HBM per device.

```python
import math
import jax
import jax.numpy as jnp
from jax import lax

S = 9
AX = 16
CA = 128
SX = 16
REACH = 64
PITCH = 256
PASSAGES = 8
NAZ = 1024
NR = 32
N_AZ = 8


def draw_inlet_index(key, part):
    key = jax.random.fold_in(key, 11)
    first_key, second_key = jax.random.split(key)
    shifts = jax.random.randint(first_key, (PASSAGES,), 1, REACH + 1)
    spreads = jax.random.randint(second_key, (PASSAGES,), 1, REACH)
    shifts = shifts.at[0].set(REACH)
    spreads = spreads.at[PASSAGES - 1].set(REACH - 1)
    lengths = CA + shifts + spreads
    columns = jnp.arange(PITCH, dtype=jnp.int32)
    return ((REACH - shifts)[:, None] + columns[None, :] * lengths[:, None] // PITCH).astype(jnp.int32)


def block_scale(key, extent, shards, low, largest):
    loudness = 1.0
    for dim, blocks in shards:
        draws = jax.random.uniform(jax.random.fold_in(jax.random.fold_in(key, 6), dim), (blocks,), jnp.float32, low / len(shards), largest / len(shards))
        loudness = loudness * jnp.repeat(jnp.exp(draws), extent[dim] // blocks).reshape((-1,) + (1,) * (len(extent) - 1 - dim))
    return loudness


def normal_values(own_key, dims, width, reach, cuts=(), held_as=jnp.bfloat16):
    values = jax.random.normal(own_key, dims, jnp.float32) * width
    if len(cuts) > 0:
        values = block_scale(own_key, dims, cuts, -0.22, 0.18) * values
    return jnp.clip(values, min=-reach, max=reach).astype(held_as)


def setup_inputs(seed: int = 0) -> dict:
    keys = jax.random.split(jax.random.key(seed), 8)
    combustor_state = normal_values(keys[0], (S, AX, NR, NAZ), 1.0, 6.0, ((2, 4), (3, 8)), jnp.float32)
    swirl_speed = jnp.clip(-0.6 + 1.6 * jax.random.uniform(keys[1], (AX, NR, NAZ), jnp.float32) ** block_scale(keys[1], (AX, NR, NAZ), ((1, 4), (2, 8)), -0.2, 0.2), -0.6, 1.0)
    reaction_rate = jnp.clip(jnp.exp(math.log(1.0) - 2.3025851 * jax.random.uniform(keys[2], (AX, NR, NAZ), jnp.float32) ** block_scale(keys[2], (AX, NR, NAZ), ((1, 4), (2, 8)), -0.2, 0.2)), 0.1, 1.0)
    kinetics = normal_values(keys[3], (S, S), S ** -0.5, 2.0, (), jnp.float32)
    stator_state = normal_values(keys[4], (S, SX, NR, PASSAGES * PITCH), 1.0, 6.0, ((2, 4), (3, 8)), jnp.float32)
    inlet_index = draw_inlet_index(jax.random.fold_in(keys[7], 71), 0)
    inlet_weight = jnp.clip(1.0 * jax.random.uniform(keys[6], (PASSAGES, PITCH), jnp.float32) ** block_scale(keys[6], (PASSAGES, PITCH), ((0, 8),), -0.2, 0.2), 0.0, 1.0)
    return dict(combustor_state=combustor_state, swirl_speed=swirl_speed, reaction_rate=reaction_rate, kinetics=kinetics, stator_state=stator_state, inlet_index=inlet_index, inlet_weight=inlet_weight)


comb_step = 0.4
axial_speed = 0.5
radial_mix = 0.25
stator_speed = 0.5
pitch_mix = 0.2
stator_mix = 0.2


def tendency(q_cycle, u_cycle, q_wall, reaction, kinetics):
    fplus = jnp.maximum(u_cycle, 0.0)[None] * q_cycle
    fminus = jnp.minimum(u_cycle, 0.0)[None] * q_cycle
    face_flux = (-fplus[..., 0:-3] + 5.0 * fplus[..., 1:-2] + 2.0 * fplus[..., 2:-1]) / 6.0 + (2.0 * fminus[..., 1:-2] + 5.0 * fminus[..., 2:-1] - fminus[..., 3:]) / 6.0
    azimuthal = face_flux[..., :-1] - face_flux[..., 1:]
    centre = q_cycle[..., 2:-2]
    before = jnp.concatenate([jnp.zeros_like(centre[:, :1]), centre[:, :-1]], axis=1)
    axial_term = axial_speed * (before - centre)
    radial = radial_mix * (q_wall[:, :, 2:] - 2.0 * centre + q_wall[:, :, :-2])
    source = reaction[None] * jnp.einsum("st,txyz->sxyz", kinetics, centre, precision=lax.Precision.HIGHEST)
    return azimuthal + axial_term + radial + source


def radial_pad(field):
    return jnp.pad(field, ((0, 0), (0, 0), (1, 1), (0, 0)))


def advance(extended, swirl_ext, reaction_ext, kinetics):
    section_one = extended[..., 2:-2] + comb_step * tendency(extended, swirl_ext, radial_pad(extended[..., 2:-2]), reaction_ext[..., 2:-2], kinetics)
    rate_two = tendency(section_one, swirl_ext[..., 2:-2], radial_pad(section_one[..., 2:-2]), reaction_ext[..., 4:-4], kinetics)
    return 0.5 * extended[..., 4:-4] + 0.5 * (section_one[..., 2:-2] + comb_step * rate_two)


def stator_update(current, below_edge, above_edge, inflow, walled):
    pitched = jnp.concatenate([below_edge, current, above_edge], axis=-1)
    before = jnp.concatenate([inflow[:, None], current[:, :-1]], axis=1)
    axial_term = stator_speed * (before - current)
    pitch_term = pitch_mix * (pitched[..., 2:] - 2.0 * current + pitched[..., :-2])
    radial = stator_mix * (walled[:, :, 2:] - 2.0 * current + walled[:, :, :-2])
    return current + (axial_term + pitch_term + radial)


def wrap_pad(field, margin):
    return jnp.concatenate([field[..., -margin:], field, field[..., :margin]], axis=-1)


def reference(combustor_state, swirl_speed, reaction_rate, kinetics, stator_state, inlet_index, inlet_weight):
    padded = wrap_pad(combustor_state, 4)
    swirl_pad = wrap_pad(swirl_speed, 4)
    rate_pad = wrap_pad(reaction_rate, 4)

    def tile_step(index):
        start = (index * CA).astype(jnp.int32)
        extended = lax.dynamic_slice_in_dim(padded, start, CA + 8, 3)
        swirl_ext = lax.dynamic_slice_in_dim(swirl_pad, start, CA + 8, 2)
        rate_ext = lax.dynamic_slice_in_dim(rate_pad, start, CA + 8, 2)
        return advance(extended, swirl_ext, rate_ext, kinetics)

    tiles = lax.map(tile_step, jnp.arange(N_AZ, dtype=jnp.int32))
    combustor_next = jnp.moveaxis(tiles, 0, 3).reshape(S, AX, NR, NAZ)
    exit_plane = combustor_next[:, AX - 1]
    ids = jnp.arange(PASSAGES, dtype=jnp.int32)

    def passage_step(passage):
        current = lax.dynamic_slice_in_dim(stator_state, (passage * PITCH).astype(jnp.int32), PITCH, 3)
        above_edge = lax.dynamic_slice_in_dim(stator_state, (((passage + 1) % PASSAGES) * PITCH).astype(jnp.int32), 1, 3)
        below_edge = lax.dynamic_slice_in_dim(stator_state, (((passage + PASSAGES - 1) % PASSAGES) * PITCH + PITCH - 1).astype(jnp.int32), 1, 3)
        left_cell = ((passage * CA - REACH + inlet_index[passage]) % NAZ).astype(jnp.int32)
        right_cell = ((left_cell + 1) % NAZ).astype(jnp.int32)
        left_value = exit_plane[:, :, left_cell]
        right_value = exit_plane[:, :, right_cell]
        weights = inlet_weight[passage]
        inflow = (1.0 - weights) * left_value + weights * right_value
        return stator_update(current, below_edge, above_edge, inflow, radial_pad(current))

    passages_out = lax.map(passage_step, ids)
    stator_next = jnp.moveaxis(passages_out, 0, 3).reshape(S, SX, NR, PASSAGES * PITCH)
    return combustor_next, stator_next
```

```python
import functools

import jax
import jax.numpy as jnp
from jax import lax
from jax.experimental import pallas as pl
from jax.experimental.pallas import tpu as pltpu
from jax.sharding import PartitionSpec as P

comb_step = 0.4
axial_speed = 0.5
radial_mix = 0.25
stator_speed = 0.5
pitch_mix = 0.2
stator_mix = 0.2

F32 = jnp.float32
BF16 = jnp.bfloat16
HI = lax.Precision.HIGHEST


def rows(tile):
    start = tile * 8
    return pl.ds(start if isinstance(start, int) else pl.multiple_of(start, 8), 8)


def split(value):
    high = value.astype(BF16)
    low = (value - high.astype(F32)).astype(BF16)
    return high, low


def kernel(
    n_az, n_rad, S, AX,
    q_hbm, u_hbm, rate_hbm, kin_hbm, st_hbm, idx_hbm, w_hbm,
    comb_out, st_out,
    q, u, rate, kin_in, sa, sb, idx, wgt,
    s1, source, coef, mat, whi, wlo, exit_x,
    edge1, edge2, exit_send, az1, az2, az3,
    row1, row2, rad1, rad2, srow, srad,
    load_sem, az_send, az_recv, rad_send, rad_recv,
):
    az = lax.axis_index("az")
    rad = lax.axis_index("rad")
    left, right = lax.rem(az + n_az - 1, n_az), lax.rem(az + 1, n_az)
    has_low, has_high = rad > 0, rad < n_rad - 1

    loads = [
        pltpu.make_async_copy(q_hbm, q, load_sem.at[0]),
        pltpu.make_async_copy(u_hbm, u, load_sem.at[1]),
        pltpu.make_async_copy(st_hbm.at[:, pl.ds(0, 128)], sa, load_sem.at[2]),
        pltpu.make_async_copy(st_hbm.at[:, pl.ds(128, 128)], sb, load_sem.at[3]),
        pltpu.make_async_copy(rate_hbm, rate, load_sem.at[4]),
        pltpu.make_async_copy(kin_hbm, kin_in, load_sem.at[5]),
        pltpu.make_async_copy(idx_hbm, idx, load_sem.at[6]),
        pltpu.make_async_copy(w_hbm, wgt, load_sem.at[7]),
    ]
    for load in loads:
        load.start()

    barrier = pltpu.get_barrier_semaphore()
    for side in (left, right):
        pl.semaphore_signal(barrier, inc=1, device_id={"az": side}, device_id_type=pl.DeviceIdType.MESH)

    @pl.when(has_low)
    def _():
        pl.semaphore_signal(barrier, inc=1, device_id={"rad": rad - 1}, device_id_type=pl.DeviceIdType.MESH)

    @pl.when(has_high)
    def _():
        pl.semaphore_signal(barrier, inc=1, device_id={"rad": rad + 1}, device_id_type=pl.DeviceIdType.MESH)

    def az_copies(phase, source_ref, landing):
        out = []
        for side, target in enumerate((left, right)):
            k = phase * 2 + side
            out.append(
                pltpu.make_async_remote_copy(
                    src_ref=source_ref,
                    dst_ref=landing.at[1 - side],
                    send_sem=az_send.at[k],
                    recv_sem=az_recv.at[phase * 2 + 1 - side],
                    device_id={"az": target},
                    device_id_type=pl.DeviceIdType.MESH,
                )
            )
        return out

    def rad_copies(phase, source_ref, landing):
        out = []
        for side, target in enumerate((rad - 1, rad + 1)):
            k = phase * 2 + side
            out.append(
                pltpu.make_async_remote_copy(
                    src_ref=source_ref.at[side],
                    dst_ref=landing.at[1 - side],
                    send_sem=rad_send.at[k],
                    recv_sem=rad_recv.at[phase * 2 + 1 - side],
                    device_id={"rad": target},
                    device_id_type=pl.DeviceIdType.MESH,
                )
            )
        return out

    def rad_each(copies, act):
        @pl.when(has_low)
        def _():
            act(copies[0], 0)

        @pl.when(has_high)
        def _():
            act(copies[1], 1)

    a1 = az_copies(0, edge1.at[pl.ds(0, (S + 1) * 8), :], az1)
    a2 = az_copies(1, edge1.at[pl.ds((S + 1) * 8, S * 8), :], az2)
    a3 = az_copies(2, exit_send, az3)
    r1 = rad_copies(0, row1, rad1)
    r2 = rad_copies(1, row2, rad2)
    r3 = rad_copies(2, srow, srad)

    def rad_wait(phase, landing):
        @pl.when(has_low)
        def _():
            pltpu.make_async_copy(landing.at[0], landing.at[0], rad_recv.at[phase * 2]).wait()

        @pl.when(has_high)
        def _():
            pltpu.make_async_copy(landing.at[1], landing.at[1], rad_recv.at[phase * 2 + 1]).wait()

    lane = lax.broadcasted_iota(jnp.int32, (8, 128), 1)
    sub = lax.broadcasted_iota(jnp.int32, (8, 128), 0)

    loads[5].wait()
    size = S * 8
    spread_c = (lax.broadcasted_iota(jnp.int32, (S, size), 1) >> 3) == lax.broadcasted_iota(jnp.int32, (S, size), 0)
    spread_r = (lax.broadcasted_iota(jnp.int32, (size, S), 0) >> 3) == lax.broadcasted_iota(jnp.int32, (size, S), 1)
    same = (lax.broadcasted_iota(jnp.int32, (size, size), 0) & 7) == (lax.broadcasted_iota(jnp.int32, (size, size), 1) & 7)
    wide = jnp.dot(kin_in[...], spread_c.astype(F32), precision=HI, preferred_element_type=F32)
    full = jnp.dot(spread_r.astype(F32), wide, precision=HI, preferred_element_type=F32)
    full = jnp.where(same, full, 0.0)
    full_hi = full.astype(BF16).astype(F32)
    mat[...] = jnp.concatenate([full_hi, full_hi, full - full_hi], axis=1).astype(BF16)

    @pl.when(jnp.logical_not(has_low))
    def _():
        for landing in (rad1, rad2, srad):
            landing[0] = jnp.zeros(landing.shape[1:], F32)

    @pl.when(jnp.logical_not(has_high))
    def _():
        for landing in (rad1, rad2, srad):
            landing[1] = jnp.zeros(landing.shape[1:], F32)

    def gather_rows(field, packed, first):
        for s in range(S):
            for side, r in ((0, 0), (1, 7)):
                packed[side, pl.ds(first + s * AX, AX), :] = field[pl.ds(s * AX * 8 + r, AX, stride=8), :]

    loads[0].wait()
    gather_rows(q, row1, 0)
    for k in (1, 2, 3):
        loads[k].wait()

    def pack_first(x, edges):
        base = x * 8
        in_q = (lane >= base) & (lane < base + 4)
        in_s = (lane >= base + 4) & (lane < base + 8)
        out = []
        for s in range(S):
            tile = s * AX + x
            a = pltpu.roll(q[rows(tile), :], base + 2, 1)
            b = pltpu.roll(jnp.where(lane == 0, sa[rows(tile), :], sb[rows(tile), :]), lax.rem(base + 5, 128), 1)
            out.append(jnp.where(in_q, a, jnp.where(in_s, b, edges[s])))
        a = pltpu.roll(u[rows(x), :], base + 2, 1)
        out.append(jnp.where(in_q, a, edges[S]))
        return tuple(out)

    zero = jnp.zeros((8, 128), F32)
    edges = lax.fori_loop(0, AX, pack_first, (zero,) * (S + 1))
    for s in range(S + 1):
        edge1[pl.ds(s * 8, 8), :] = edges[s]

    n_wait = 2 + has_low.astype(jnp.int32) + has_high.astype(jnp.int32)
    pl.semaphore_wait(barrier, n_wait)
    rad_each(r1, lambda c, side: c.start())
    for c in a1:
        c.start()
    gather_rows(sa, srow, 0)
    gather_rows(sb, srow, S * AX)
    rad_each(r3, lambda c, side: c.start())

    loads[6].wait()
    loads[7].wait()
    place = (lax.broadcasted_iota(jnp.int32, (256, 256), 0) + 64) & 255
    first = idx[...]
    w = wgt[...]
    weights = jnp.where(place == first, 1.0 - w, 0.0) + jnp.where(place == first + 1, w, 0.0)
    weights_hi, weights_lo = split(weights)
    whi[...] = weights_hi
    wlo[...] = weights_lo

    def react(field):
        def step(x, carry):
            tiles = [field[rows(s * AX + x), :] for s in range(S)]
            highs = [t.astype(BF16).astype(F32) for t in tiles]
            lows = [t - h for t, h in zip(tiles, highs)]
            stack = jnp.concatenate(highs + lows + highs, axis=0).astype(BF16)
            source[pl.ds(pl.multiple_of(x * size, 8), size), :] = jnp.dot(
                mat[...], stack, preferred_element_type=F32
            )
            return carry

        lax.fori_loop(0, AX, step, 0, unroll=4)

    react(q)
    loads[4].wait()
    for c in a1:
        c.wait_recv()

    from_left = ((lane & 7) < 2) | ((lane & 7) == 4)

    def merged(landing, s):
        return jnp.where(from_left, landing[0, pl.ds(s * 8, 8), :], landing[1, pl.ds(s * 8, 8), :])

    for s in range(S + 1):
        edge2[pl.ds(s * 8, 8), :] = merged(az1, s)

    def shifts(tile, halo):
        m2 = pltpu.roll(jnp.where(lane >= 126, halo, tile), 2, 1)
        m1 = pltpu.roll(jnp.where(lane == 127, halo, tile), 1, 1)
        p1 = pltpu.roll(jnp.where(lane == 0, halo, tile), 127, 1)
        p2 = pltpu.roll(jnp.where(lane < 2, halo, tile), 126, 1)
        return m2, m1, p1, p2

    def coefficients(x, carry):
        here = u[rows(x), :]
        halo = pltpu.roll(edge2[pl.ds(S * 8, 8), :], 126 - x * 8, 1)
        m2, m1, p1, p2 = shifts(here, halo)
        base = x * 6
        coef[rows(base), :] = jnp.maximum(m2, 0.0) * (-comb_step / 6.0)
        coef[rows(base + 1), :] = comb_step * jnp.maximum(m1, 0.0) + (comb_step / 3.0) * jnp.minimum(m1, 0.0)
        coef[rows(base + 2), :] = (1.0 - comb_step * (axial_speed + 2.0 * radial_mix)) - (0.5 * comb_step) * jnp.abs(here)
        coef[rows(base + 3), :] = (-comb_step / 3.0) * jnp.maximum(p1, 0.0) - comb_step * jnp.minimum(p1, 0.0)
        coef[rows(base + 4), :] = (comb_step / 6.0) * jnp.minimum(p2, 0.0)
        coef[rows(base + 5), :] = comb_step * rate[rows(x), :]
        return carry

    lax.fori_loop(0, AX, coefficients, 0)

    def advance(field, rims, walls, s, x, scale):
        tile = s * AX + x
        here = field[rows(tile), :]
        halo = pltpu.roll(rims[pl.ds(s * 8, 8), :], 126 - x * 8, 1)
        m2, m1, p1, p2 = shifts(here, halo)
        before = field[rows(s * AX + jnp.maximum(x - 1, 0)), :]
        down = jnp.where(sub == 0, walls[0, pl.ds(tile, 1), :], pltpu.roll(here, 1, 0))
        up = jnp.where(sub == 7, walls[1, pl.ds(tile, 1), :], pltpu.roll(here, 7, 0))
        base = x * 6
        total = coef[rows(base), :] * m2 + coef[rows(base + 1), :] * m1
        total += coef[rows(base + 2), :] * here
        total += coef[rows(base + 3), :] * p1 + coef[rows(base + 4), :] * p2
        total += coef[rows(base + 5), :] * source[rows(x * S + s), :]
        return total + scale * before + (comb_step * radial_mix) * (down + up)

    def upwind(x):
        return jnp.where(x > 0, comb_step * axial_speed, 0.0)

    rad_wait(0, rad1)

    def section_one(x, edges):
        scale = upwind(x)
        base = x * 8
        inside = (lane >= base) & (lane < base + 4)
        out = []
        for s in range(S):
            value = advance(q, edge2, rad1, s, x, scale)
            s1[rows(s * AX + x), :] = value
            out.append(jnp.where(inside, pltpu.roll(value, base + 2, 1), edges[s]))
        return tuple(out)

    edges = lax.fori_loop(0, AX, section_one, (zero,) * S)
    for s in range(S):
        edge1[pl.ds((S + 1 + s) * 8, 8), :] = edges[s]
    gather_rows(s1, row2, 0)
    rad_each(r2, lambda c, side: c.start())
    for c in a2:
        c.start()

    react(s1)
    rad_wait(2, srad)

    def passage(x, carry):
        scale = jnp.where(x > 0, stator_speed, 0.0)
        for s in range(S):
            tile = s * AX + x
            a = sa[rows(tile), :]
            b = sb[rows(tile), :]
            halo = pltpu.roll(edge2[pl.ds(s * 8, 8), :], lax.rem(123 - x * 8 + 128, 128), 1)
            a_left = pltpu.roll(jnp.where(lane == 127, halo, a), 1, 1)
            a_right = pltpu.roll(jnp.where(lane == 0, b, a), 127, 1)
            b_left = pltpu.roll(jnp.where(lane == 127, a, b), 1, 1)
            b_right = pltpu.roll(jnp.where(lane == 0, halo, b), 127, 1)
            old = s * AX + jnp.maximum(x - 1, 0)
            for k, (here, lft, rgt, field) in enumerate(((a, a_left, a_right, sa), (b, b_left, b_right, sb))):
                part = pl.ds(k * 128, 128)
                down = jnp.where(sub == 0, srad[0, pl.ds(k * S * AX + tile, 1), :], pltpu.roll(here, 1, 0))
                up = jnp.where(sub == 7, srad[1, pl.ds(k * S * AX + tile, 1), :], pltpu.roll(here, 7, 0))
                st_out[rows(tile), part] = (
                    (1.0 - stator_speed - 2.0 * pitch_mix - 2.0 * stator_mix) * here
                    + scale * field[rows(old), :]
                    + pitch_mix * (lft + rgt)
                    + stator_mix * (down + up)
                )
        return carry

    lax.fori_loop(0, AX, passage, 0)

    for c in a2:
        c.wait_recv()
    rad_wait(1, rad2)
    for s in range(S):
        exit_x[pl.ds(s * 8, 8), :] = merged(az2, s)

    def section_two(x):
        scale = upwind(x)
        for s in range(S):
            tile = s * AX + x
            value = 0.5 * (q[rows(tile), :] + advance(s1, exit_x, rad2, s, x, scale))
            comb_out[rows(tile), :] = value
            yield s, value

    for s, value in section_two(AX - 1):
        exit_send[pl.ds(s * 8, 8), :] = value
    for c in a3:
        c.start()

    def rest(x, carry):
        for _ in section_two(x):
            pass
        return carry

    lax.fori_loop(0, AX - 1, rest, 0)

    own = exit_send[...]
    for c in a3:
        c.wait_recv()
    wide_lane = lax.broadcasted_iota(jnp.int32, (size, 128), 1)
    rim = jnp.where(wide_lane < 64, az3[1], az3[0])
    cells = jnp.concatenate([own, rim], axis=1)
    cells_hi, cells_lo = split(cells)
    inflow = jnp.dot(cells_hi, whi[...], preferred_element_type=F32)
    inflow += jnp.dot(cells_lo, whi[...], preferred_element_type=F32)
    inflow += jnp.dot(cells_hi, wlo[...], preferred_element_type=F32)
    for s in range(S):
        st_out[rows(s * AX), :] += stator_speed * inflow[s * 8 : s * 8 + 8, :]

    for c in a1 + a2 + a3:
        c.wait_send()
    for copies in (r1, r2, r3):
        rad_each(copies, lambda c, side: c.wait_send())


def body(
    n_az, n_rad, combustor_state, swirl_speed, reaction_rate, kinetics, stator_state, inlet_index, inlet_weight
):
    S, AX, NR, CA = combustor_state.shape
    pitch = stator_state.shape[3]
    tiles = S * AX
    VM = pltpu.VMEM
    dma = pltpu.SemaphoreType.DMA
    any_spec = pl.BlockSpec(memory_space=pl.ANY)
    comb, stator = pl.pallas_call(
        functools.partial(kernel, n_az, n_rad, S, AX),
        out_shape=(
            jax.ShapeDtypeStruct((tiles * 8, 128), F32),
            jax.ShapeDtypeStruct((tiles * 8, 256), F32),
        ),
        in_specs=[any_spec] * 7,
        out_specs=(pl.BlockSpec(memory_space=VM), pl.BlockSpec(memory_space=VM)),
        scratch_shapes=[
            VM((tiles * 8, 128), F32),
            VM((AX * 8, 128), F32),
            VM((AX * 8, 128), F32),
            VM((S, S), F32),
            VM((tiles * 8, 128), F32),
            VM((tiles * 8, 128), F32),
            VM((1, 256), jnp.int32),
            VM((1, 256), F32),
            VM((tiles * 8, 128), F32),
            VM((tiles * 8, 128), F32),
            VM((AX * 6 * 8, 128), F32),
            VM((S * 8, S * 24), BF16),
            VM((256, 256), BF16),
            VM((256, 256), BF16),
            VM((S * 8, 128), F32),
            VM(((2 * S + 1) * 8, 128), F32),
            VM(((S + 1) * 8, 128), F32),
            VM((S * 8, 128), F32),
            VM((2, (S + 1) * 8, 128), F32),
            VM((2, S * 8, 128), F32),
            VM((2, S * 8, 128), F32),
            VM((2, tiles, 128), F32),
            VM((2, tiles, 128), F32),
            VM((2, tiles, 128), F32),
            VM((2, tiles, 128), F32),
            VM((2, 2 * tiles, 128), F32),
            VM((2, 2 * tiles, 128), F32),
            dma((8,)),
            dma((6,)),
            dma((6,)),
            dma((6,)),
            dma((6,)),
        ],
        compiler_params=pltpu.CompilerParams(
            collective_id=0, has_side_effects=True, vmem_limit_bytes=40 * 1024 * 1024
        ),
        cost_estimate=pl.CostEstimate(flops=40000000, bytes_accessed=4000000, transcendentals=0),
    )(
        combustor_state.reshape(tiles * NR, CA),
        swirl_speed.reshape(AX * NR, CA),
        reaction_rate.reshape(AX * NR, CA),
        kinetics,
        stator_state.reshape(tiles * NR, pitch),
        inlet_index,
        inlet_weight,
    )
    return (comb.reshape(combustor_state.shape), stator.reshape(stator_state.shape))


def solution(mesh):
    in_specs = (
        P(None, None, "rad", "az"),
        P(None, "rad", "az"),
        P(None, "rad", "az"),
        P(),
        P(None, None, "rad", "az"),
        P("az", None),
        P("az", None),
    )
    out_specs = (P(None, None, "rad", "az"), P(None, None, "rad", "az"))
    return jax.shard_map(
        functools.partial(body, mesh.shape["az"], mesh.shape["rad"]),
        mesh=mesh,
        in_specs=in_specs,
        out_specs=out_specs,
        check_vma=False,
    )
```

```python
import functools

import jax
import jax.numpy as jnp
from jax import lax
from jax.experimental import pallas as pl
from jax.experimental.pallas import tpu as pltpu
from jax.sharding import PartitionSpec as P

comb_step = 0.4
axial_speed = 0.5
radial_mix = 0.25
stator_speed = 0.5
pitch_mix = 0.2
stator_mix = 0.2

F32 = jnp.float32
BF16 = jnp.bfloat16
HI = lax.Precision.HIGHEST


def rows(tile):
    start = tile * 8
    return pl.ds(start if isinstance(start, int) else pl.multiple_of(start, 8), 8)


def split(value):
    high = value.astype(BF16)
    low = (value - high.astype(F32)).astype(BF16)
    return high, low


def kernel(
    n_az, n_rad, S, AX,
    q_hbm, u_hbm, rate_hbm, kin_hbm, st_hbm, idx_hbm, w_hbm,
    comb_out, st_out,
    q, u, rate, kin_in, sa, sb, idx, wgt,
    s1, source, coef, mat, whi, wlo, exit_x,
    edge1, edge2, exit_send, az1, az2, az3,
    row1, row2, rad1, rad2, srow, srad,
    load_sem, az_send, az_recv, rad_send, rad_recv,
):
    az = lax.axis_index("az")
    rad = lax.axis_index("rad")
    left, right = lax.rem(az + n_az - 1, n_az), lax.rem(az + 1, n_az)
    has_low, has_high = rad > 0, rad < n_rad - 1

    loads = [
        pltpu.make_async_copy(q_hbm, q, load_sem.at[0]),
        pltpu.make_async_copy(u_hbm, u, load_sem.at[1]),
        pltpu.make_async_copy(st_hbm.at[:, pl.ds(0, 128)], sa, load_sem.at[2]),
        pltpu.make_async_copy(st_hbm.at[:, pl.ds(128, 128)], sb, load_sem.at[3]),
        pltpu.make_async_copy(rate_hbm, rate, load_sem.at[4]),
        pltpu.make_async_copy(kin_hbm, kin_in, load_sem.at[5]),
        pltpu.make_async_copy(idx_hbm, idx, load_sem.at[6]),
        pltpu.make_async_copy(w_hbm, wgt, load_sem.at[7]),
    ]
    for load in loads:
        load.start()

    barrier = pltpu.get_barrier_semaphore()
    for side in (left, right):
        pl.semaphore_signal(barrier, inc=1, device_id={"az": side}, device_id_type=pl.DeviceIdType.MESH)

    @pl.when(has_low)
    def _():
        pl.semaphore_signal(barrier, inc=1, device_id={"rad": rad - 1}, device_id_type=pl.DeviceIdType.MESH)

    @pl.when(has_high)
    def _():
        pl.semaphore_signal(barrier, inc=1, device_id={"rad": rad + 1}, device_id_type=pl.DeviceIdType.MESH)

    def az_copies(phase, source_ref, landing):
        out = []
        for side, target in enumerate((left, right)):
            k = phase * 2 + side
            out.append(
                pltpu.make_async_remote_copy(
                    src_ref=source_ref,
                    dst_ref=landing.at[1 - side],
                    send_sem=az_send.at[k],
                    recv_sem=az_recv.at[phase * 2 + 1 - side],
                    device_id={"az": target},
                    device_id_type=pl.DeviceIdType.MESH,
                )
            )
        return out

    def rad_copies(phase, source_ref, landing):
        out = []
        for side, target in enumerate((rad - 1, rad + 1)):
            k = phase * 2 + side
            out.append(
                pltpu.make_async_remote_copy(
                    src_ref=source_ref.at[side],
                    dst_ref=landing.at[1 - side],
                    send_sem=rad_send.at[k],
                    recv_sem=rad_recv.at[phase * 2 + 1 - side],
                    device_id={"rad": target},
                    device_id_type=pl.DeviceIdType.MESH,
                )
            )
        return out

    def rad_each(copies, act):
        @pl.when(has_low)
        def _():
            act(copies[0], 0)

        @pl.when(has_high)
        def _():
            act(copies[1], 1)

    a1 = az_copies(0, edge1.at[pl.ds(0, (S + 1) * 8), :], az1)
    a2 = az_copies(1, edge1.at[pl.ds((S + 1) * 8, S * 8), :], az2)
    a3 = az_copies(2, exit_send, az3)
    r1 = rad_copies(0, row1, rad1)
    r2 = rad_copies(1, row2, rad2)
    r3 = rad_copies(2, srow, srad)

    def rad_wait(phase, landing):
        @pl.when(has_low)
        def _():
            pltpu.make_async_copy(landing.at[0], landing.at[0], rad_recv.at[phase * 2]).wait()

        @pl.when(has_high)
        def _():
            pltpu.make_async_copy(landing.at[1], landing.at[1], rad_recv.at[phase * 2 + 1]).wait()

    lane = lax.broadcasted_iota(jnp.int32, (8, 128), 1)
    sub = lax.broadcasted_iota(jnp.int32, (8, 128), 0)

    loads[5].wait()
    size = S * 8
    spread_c = (lax.broadcasted_iota(jnp.int32, (S, size), 1) >> 3) == lax.broadcasted_iota(jnp.int32, (S, size), 0)
    spread_r = (lax.broadcasted_iota(jnp.int32, (size, S), 0) >> 3) == lax.broadcasted_iota(jnp.int32, (size, S), 1)
    same = (lax.broadcasted_iota(jnp.int32, (size, size), 0) & 7) == (lax.broadcasted_iota(jnp.int32, (size, size), 1) & 7)
    wide = jnp.dot(kin_in[...], spread_c.astype(F32), precision=HI, preferred_element_type=F32)
    full = jnp.dot(spread_r.astype(F32), wide, precision=HI, preferred_element_type=F32)
    full = jnp.where(same, full, 0.0)
    full_hi = full.astype(BF16).astype(F32)
    mat[...] = jnp.concatenate([full_hi, full_hi, full - full_hi], axis=1).astype(BF16)

    @pl.when(jnp.logical_not(has_low))
    def _():
        for landing in (rad1, rad2, srad):
            landing[0] = jnp.zeros(landing.shape[1:], F32)

    @pl.when(jnp.logical_not(has_high))
    def _():
        for landing in (rad1, rad2, srad):
            landing[1] = jnp.zeros(landing.shape[1:], F32)

    def gather_rows(field, packed, first):
        for s in range(S):
            for side, r in ((0, 0), (1, 7)):
                packed[side, pl.ds(first + s * AX, AX), :] = field[pl.ds(s * AX * 8 + r, AX, stride=8), :]

    loads[0].wait()
    gather_rows(q, row1, 0)
    for k in (1, 2, 3):
        loads[k].wait()

    def pack_first(x, edges):
        base = x * 8
        in_q = (lane >= base) & (lane < base + 4)
        in_s = (lane >= base + 4) & (lane < base + 8)
        out = []
        for s in range(S):
            tile = s * AX + x
            a = pltpu.roll(q[rows(tile), :], base + 2, 1)
            b = pltpu.roll(jnp.where(lane == 0, sa[rows(tile), :], sb[rows(tile), :]), lax.rem(base + 5, 128), 1)
            out.append(jnp.where(in_q, a, jnp.where(in_s, b, edges[s])))
        a = pltpu.roll(u[rows(x), :], base + 2, 1)
        out.append(jnp.where(in_q, a, edges[S]))
        return tuple(out)

    zero = jnp.zeros((8, 128), F32)
    edges = lax.fori_loop(0, AX, pack_first, (zero,) * (S + 1), unroll=2)
    for s in range(S + 1):
        edge1[pl.ds(s * 8, 8), :] = edges[s]

    n_wait = 2 + has_low.astype(jnp.int32) + has_high.astype(jnp.int32)
    pl.semaphore_wait(barrier, n_wait)
    rad_each(r1, lambda c, side: c.start())
    for c in a1:
        c.start()
    gather_rows(sa, srow, 0)
    gather_rows(sb, srow, S * AX)
    rad_each(r3, lambda c, side: c.start())

    loads[6].wait()
    loads[7].wait()
    place = (lax.broadcasted_iota(jnp.int32, (256, 256), 0) + 64) & 255
    first = idx[...]
    w = wgt[...]
    weights = jnp.where(place == first, 1.0 - w, 0.0) + jnp.where(place == first + 1, w, 0.0)
    weights_hi, weights_lo = split(weights)
    whi[...] = weights_hi
    wlo[...] = weights_lo

    def react(field):
        def step(x, carry):
            tiles = [field[rows(s * AX + x), :] for s in range(S)]
            highs = [t.astype(BF16).astype(F32) for t in tiles]
            lows = [t - h for t, h in zip(tiles, highs)]
            stack = jnp.concatenate(highs + lows + highs, axis=0).astype(BF16)
            source[pl.ds(pl.multiple_of(x * size, 8), size), :] = jnp.dot(
                mat[...], stack, preferred_element_type=F32
            )
            return carry

        lax.fori_loop(0, AX, step, 0, unroll=16)

    react(q)
    loads[4].wait()
    for c in a1:
        c.wait_recv()

    from_left = ((lane & 7) < 2) | ((lane & 7) == 4)

    def merged(landing, s):
        return jnp.where(from_left, landing[0, pl.ds(s * 8, 8), :], landing[1, pl.ds(s * 8, 8), :])

    for s in range(S + 1):
        edge2[pl.ds(s * 8, 8), :] = merged(az1, s)

    def shifts(tile, halo):
        m2 = pltpu.roll(jnp.where(lane >= 126, halo, tile), 2, 1)
        m1 = pltpu.roll(jnp.where(lane == 127, halo, tile), 1, 1)
        p1 = pltpu.roll(jnp.where(lane == 0, halo, tile), 127, 1)
        p2 = pltpu.roll(jnp.where(lane < 2, halo, tile), 126, 1)
        return m2, m1, p1, p2

    def coefficients(x, carry):
        here = u[rows(x), :]
        halo = pltpu.roll(edge2[pl.ds(S * 8, 8), :], 126 - x * 8, 1)
        m2, m1, p1, p2 = shifts(here, halo)
        base = x * 6
        coef[rows(base), :] = jnp.maximum(m2, 0.0) * (-comb_step / 6.0)
        coef[rows(base + 1), :] = comb_step * jnp.maximum(m1, 0.0) + (comb_step / 3.0) * jnp.minimum(m1, 0.0)
        coef[rows(base + 2), :] = (1.0 - comb_step * (axial_speed + 2.0 * radial_mix)) - (0.5 * comb_step) * jnp.abs(here)
        coef[rows(base + 3), :] = (-comb_step / 3.0) * jnp.maximum(p1, 0.0) - comb_step * jnp.minimum(p1, 0.0)
        coef[rows(base + 4), :] = (comb_step / 6.0) * jnp.minimum(p2, 0.0)
        coef[rows(base + 5), :] = comb_step * rate[rows(x), :]
        return carry

    lax.fori_loop(0, AX, coefficients, 0, unroll=4)

    def advance(field, rims, walls, s, x, scale):
        tile = s * AX + x
        here = field[rows(tile), :]
        halo = pltpu.roll(rims[pl.ds(s * 8, 8), :], 126 - x * 8, 1)
        m2, m1, p1, p2 = shifts(here, halo)
        before = field[rows(s * AX + jnp.maximum(x - 1, 0)), :]
        down = jnp.where(sub == 0, walls[0, pl.ds(tile, 1), :], pltpu.roll(here, 1, 0))
        up = jnp.where(sub == 7, walls[1, pl.ds(tile, 1), :], pltpu.roll(here, 7, 0))
        base = x * 6
        total = coef[rows(base), :] * m2 + coef[rows(base + 1), :] * m1
        total += coef[rows(base + 2), :] * here
        total += coef[rows(base + 3), :] * p1 + coef[rows(base + 4), :] * p2
        total += coef[rows(base + 5), :] * source[rows(x * S + s), :]
        return total + scale * before + (comb_step * radial_mix) * (down + up)

    def upwind(x):
        return jnp.where(x > 0, comb_step * axial_speed, 0.0)

    rad_wait(0, rad1)

    def section_one(x, edges):
        scale = upwind(x)
        base = x * 8
        inside = (lane >= base) & (lane < base + 4)
        out = []
        for s in range(S):
            value = advance(q, edge2, rad1, s, x, scale)
            s1[rows(s * AX + x), :] = value
            out.append(jnp.where(inside, pltpu.roll(value, base + 2, 1), edges[s]))
        return tuple(out)

    edges = lax.fori_loop(0, AX, section_one, (zero,) * S, unroll=2)
    for s in range(S):
        edge1[pl.ds((S + 1 + s) * 8, 8), :] = edges[s]
    gather_rows(s1, row2, 0)
    rad_each(r2, lambda c, side: c.start())
    for c in a2:
        c.start()

    react(s1)
    rad_wait(2, srad)

    def passage(x, carry):
        scale = jnp.where(x > 0, stator_speed, 0.0)
        for s in range(S):
            tile = s * AX + x
            a = sa[rows(tile), :]
            b = sb[rows(tile), :]
            halo = pltpu.roll(edge2[pl.ds(s * 8, 8), :], lax.rem(123 - x * 8 + 128, 128), 1)
            a_left = pltpu.roll(jnp.where(lane == 127, halo, a), 1, 1)
            a_right = pltpu.roll(jnp.where(lane == 0, b, a), 127, 1)
            b_left = pltpu.roll(jnp.where(lane == 127, a, b), 1, 1)
            b_right = pltpu.roll(jnp.where(lane == 0, halo, b), 127, 1)
            old = s * AX + jnp.maximum(x - 1, 0)
            for k, (here, lft, rgt, field) in enumerate(((a, a_left, a_right, sa), (b, b_left, b_right, sb))):
                part = pl.ds(k * 128, 128)
                down = jnp.where(sub == 0, srad[0, pl.ds(k * S * AX + tile, 1), :], pltpu.roll(here, 1, 0))
                up = jnp.where(sub == 7, srad[1, pl.ds(k * S * AX + tile, 1), :], pltpu.roll(here, 7, 0))
                st_out[rows(tile), part] = (
                    (1.0 - stator_speed - 2.0 * pitch_mix - 2.0 * stator_mix) * here
                    + scale * field[rows(old), :]
                    + pitch_mix * (lft + rgt)
                    + stator_mix * (down + up)
                )
        return carry

    lax.fori_loop(0, AX, passage, 0, unroll=2)

    for c in a2:
        c.wait_recv()
    rad_wait(1, rad2)
    for s in range(S):
        exit_x[pl.ds(s * 8, 8), :] = merged(az2, s)

    def section_two(x):
        scale = upwind(x)
        for s in range(S):
            tile = s * AX + x
            value = 0.5 * (q[rows(tile), :] + advance(s1, exit_x, rad2, s, x, scale))
            comb_out[rows(tile), :] = value
            yield s, value

    for s, value in section_two(AX - 1):
        exit_send[pl.ds(s * 8, 8), :] = value
    for c in a3:
        c.start()

    def rest(x, carry):
        for _ in section_two(x):
            pass
        return carry

    lax.fori_loop(0, AX - 1, rest, 0, unroll=3)

    own = exit_send[...]
    for c in a3:
        c.wait_recv()
    wide_lane = lax.broadcasted_iota(jnp.int32, (size, 128), 1)
    rim = jnp.where(wide_lane < 64, az3[1], az3[0])
    cells = jnp.concatenate([own, rim], axis=1)
    cells_hi, cells_lo = split(cells)
    inflow = jnp.dot(cells_hi, whi[...], preferred_element_type=F32)
    inflow += jnp.dot(cells_lo, whi[...], preferred_element_type=F32)
    inflow += jnp.dot(cells_hi, wlo[...], preferred_element_type=F32)
    for s in range(S):
        st_out[rows(s * AX), :] += stator_speed * inflow[s * 8 : s * 8 + 8, :]

    for c in a1 + a2 + a3:
        c.wait_send()
    for copies in (r1, r2, r3):
        rad_each(copies, lambda c, side: c.wait_send())


def body(
    n_az, n_rad, combustor_state, swirl_speed, reaction_rate, kinetics, stator_state, inlet_index, inlet_weight
):
    S, AX, NR, CA = combustor_state.shape
    pitch = stator_state.shape[3]
    tiles = S * AX
    VM = pltpu.VMEM
    dma = pltpu.SemaphoreType.DMA
    any_spec = pl.BlockSpec(memory_space=pl.ANY)
    comb, stator = pl.pallas_call(
        functools.partial(kernel, n_az, n_rad, S, AX),
        out_shape=(
            jax.ShapeDtypeStruct((tiles * 8, 128), F32),
            jax.ShapeDtypeStruct((tiles * 8, 256), F32),
        ),
        in_specs=[any_spec] * 7,
        out_specs=(pl.BlockSpec(memory_space=VM), pl.BlockSpec(memory_space=VM)),
        scratch_shapes=[
            VM((tiles * 8, 128), F32),
            VM((AX * 8, 128), F32),
            VM((AX * 8, 128), F32),
            VM((S, S), F32),
            VM((tiles * 8, 128), F32),
            VM((tiles * 8, 128), F32),
            VM((1, 256), jnp.int32),
            VM((1, 256), F32),
            VM((tiles * 8, 128), F32),
            VM((tiles * 8, 128), F32),
            VM((AX * 6 * 8, 128), F32),
            VM((S * 8, S * 24), BF16),
            VM((256, 256), BF16),
            VM((256, 256), BF16),
            VM((S * 8, 128), F32),
            VM(((2 * S + 1) * 8, 128), F32),
            VM(((S + 1) * 8, 128), F32),
            VM((S * 8, 128), F32),
            VM((2, (S + 1) * 8, 128), F32),
            VM((2, S * 8, 128), F32),
            VM((2, S * 8, 128), F32),
            VM((2, tiles, 128), F32),
            VM((2, tiles, 128), F32),
            VM((2, tiles, 128), F32),
            VM((2, tiles, 128), F32),
            VM((2, 2 * tiles, 128), F32),
            VM((2, 2 * tiles, 128), F32),
            dma((8,)),
            dma((6,)),
            dma((6,)),
            dma((6,)),
            dma((6,)),
        ],
        compiler_params=pltpu.CompilerParams(
            collective_id=0, has_side_effects=True, vmem_limit_bytes=58 * 1024 * 1024
        ),
        cost_estimate=pl.CostEstimate(flops=40000000, bytes_accessed=4000000, transcendentals=0),
    )(
        combustor_state.reshape(tiles * NR, CA),
        swirl_speed.reshape(AX * NR, CA),
        reaction_rate.reshape(AX * NR, CA),
        kinetics,
        stator_state.reshape(tiles * NR, pitch),
        inlet_index,
        inlet_weight,
    )
    return (comb.reshape(combustor_state.shape), stator.reshape(stator_state.shape))


def solution(mesh):
    in_specs = (
        P(None, None, "rad", "az"),
        P(None, "rad", "az"),
        P(None, "rad", "az"),
        P(),
        P(None, None, "rad", "az"),
        P("az", None),
        P("az", None),
    )
    out_specs = (P(None, None, "rad", "az"), P(None, None, "rad", "az"))
    return jax.shard_map(
        functools.partial(body, mesh.shape["az"], mesh.shape["rad"]),
        mesh=mesh,
        in_specs=in_specs,
        out_specs=out_specs,
        check_vma=False,
    )
```
